32 devices in a mesh: seq: 8 (over y, x, core), vocab: 4 (over z).
Axes of the slice: x: 2, y: 2, z: 4, core: 2. Of those that a mesh axis runs over, the one named last changes fastest.
Arguments:
- hidden: bfloat16 [2, 4096, 2048], P(None, 'seq'), may hold values from -6 to 6
- w_inner: bfloat16 [2, 2048, 2, 4096], P(None, None, None, 'vocab'), may hold values from -0.125 to 0.125
- w_state: bfloat16 [2, 2048, 2, 128], replicated, may hold values from -0.125 to 0.125
- w_step: bfloat16 [2, 2048, 64], P(None, None, 'vocab'), may hold values from -0.125 to 0.125
- step_bias: float32 [2, 64], P(None, 'vocab'), may hold values from -5 to -2
- rate: float32 [2, 64], P(None, 'vocab'), may hold values from 0.01 to 1.5
- skip_gain: float32 [2, 64], P(None, 'vocab'), may hold values from 0.5 to 1.5
- norm_gain: float32 [2, 4096], P(None, 'vocab'), may hold values from 0.1 to 1.9
- w_out: bfloat16 [2, 4096, 2048], P(None, 'vocab'), may hold values from -0.09375 to 0.09375
- final_gain: float32 [2, 2048], replicated, may hold values from 0.1 to 1.9
- head: bfloat16 [2, 2048, 26624], P(None, None, 'vocab'), as said below
- pool: bfloat16 [2, 16, 64, 64, 128], P(None, None, 'vocab'), may hold values from -3 to 3
- targets: int32 [4096], P('seq'), may hold values from 0 to 26623
- segment_ids: int32 [4096], P('seq'), may hold values from 0 to 3, never falling along the last dimension, each value on 1 to 2048 neighbouring positions
- flags: int32 [4], replicated, may hold values from 0 to 1, as said below
- pages: int32 [4], replicated, may hold values from 0 to 15
- live: int32 [16], P('seq'), may hold values 0 or 1
- owners: int32 [4], replicated, may hold values from 0 to 7
Outputs:
- token_diff: float32 [4096], P('seq')
- owned: float32 [8, 4], P('seq')
The draws below stay inside these ranges and needn't reach their ends.
Inputs may be any that keep to these rules, and one draw needn't show every extreme that they name: `segment_ids`: ids never fall along the positions, and every id from 0 to 3 occurs. `flags`: exactly one sequence has flag 0. `head`: each vocabulary column's entries are normal with a scale between 3 and 30 over the square root of 2048.
All inputs are finite; a program needn't handle non-finite values. No bound on the sum of `live` on one device may be relied on, other than what follows from the above.
Results may differ from the reference program's by a relative error of at most 0.029.
Values may be sent and summed in bfloat16 or wider, within the bound.
A program may use at most 192 MiB of HBM per device.

```python
import math
import jax
import jax.numpy as jnp
import numpy as np
from jax import lax

D = 2048
HEADS = 64
HEAD_DIM = 64
INNER = 4096
STATE = 128
SPAN = 256
VOCAB = 26624
PAGES = 16
TOKENS = 4096
NSEQ = 4
MAXLEN = 2048
NBLK = 16
N_SEQ = 8
N_VOCAB = 4


def draw_head(key, part):
    normal_key = jax.random.fold_in(jax.random.fold_in(key, 11), 0)
    values = jax.random.normal(normal_key, (2, D, VOCAB), jnp.float32) * (3.0 / math.sqrt(D))
    return values.astype(jnp.bfloat16)


def draw_flags(key, part):
    fresh = jax.random.randint(jax.random.fold_in(key, 23), (), 0, NSEQ, jnp.int32)
    return (jnp.arange(NSEQ, dtype=jnp.int32) != fresh).astype(jnp.int32)


def with_ends(result, stream_key, least, high):
    longest = result.shape.index(max(result.shape))
    spots = []
    for shift in (0, 1):
        where = [jax.random.randint(jax.random.fold_in(stream_key, axis), (), 0, length) for axis, length in enumerate(result.shape)]
        where[longest] = (where[longest] + shift) % result.shape[longest]
        spots.append(tuple(where))
    return result.at[spots[0]].set(least).at[spots[1]].set(high)


def steps_of(stream_key, shape, cuts, least, top_value):
    level, own = 1.0, jax.random.fold_in(stream_key, 6)
    for axis_at, blocks in cuts:
        draws = jnp.exp(jax.random.uniform(jax.random.fold_in(own, axis_at), (blocks,), jnp.float32, least / len(cuts), top_value / len(cuts)))
        level = level * jnp.repeat(draws, shape[axis_at] // blocks).reshape([-1 if axis == axis_at else 1 for axis in range(len(shape))])
    return level


def rank_bounds(number_of, lean):
    loads = [(1 << 20) // math.isqrt(standing ** lean) + 1 for standing in range(1, number_of + 1)]
    width = 1 + sum(loads) // (1 << 30)
    return np.cumsum(np.array([max(1, weight // width) for weight in loads]))


def ranked_ids(stream_key, dims, count, lean):
    grid = rank_bounds(count, lean)
    lot = jax.random.randint(jax.random.fold_in(stream_key, 1), dims, 0, int(grid[count - 1]))
    standing = jnp.searchsorted(jnp.asarray(grid, jnp.int32), lot, side="right")
    return jax.random.permutation(jax.random.fold_in(stream_key, 2), count)[standing].astype(jnp.int32)


def length_profile(number_of, total, most, slope):
    loads = [(1 << 20) // math.isqrt(standing ** slope) + 1 for standing in range(2, number_of + 1)]
    rest, counts = total - most - (number_of - 1), [1] * (number_of - 1)
    while rest > 0:
        movable = [i for i in range(number_of - 1) if counts[i] < most]
        whole, remaining = sum([loads[i] for i in movable]), rest
        for i in movable:
            addition = min(most - counts[i], max(1, remaining * loads[i] // whole), rest)
            counts[i] = counts[i] + addition
            rest = rest - addition
    return np.array([most] + counts)


def ragged_sizes(key, number_of, total, bound, skew):
    if number_of == 2:
        one = jax.random.randint(key, (), max(1, total - bound), min(bound, total - 1) + 1)
        return jnp.stack([one, total - one])
    tallies = jnp.asarray(length_profile(number_of, total, bound, skew), jnp.int32)
    pairs = (number_of - 1) // 2
    giver, receiver = tallies[1:1 + 2 * pairs:2], tallies[2:2 + 2 * pairs:2]
    room = jnp.minimum(giver - 1, bound - receiver)
    moved = jax.random.randint(jax.random.fold_in(key, 1), (pairs,), 0, 1 << 20) % (room + 1)
    tallies = tallies.at[1:1 + 2 * pairs:2].set(giver - moved).at[2:2 + 2 * pairs:2].set(receiver + moved)
    return tallies[jax.random.permutation(jax.random.fold_in(key, 2), number_of)]


def normal_values(rng, dims, deviation, reach, cuts=(), kind=jnp.bfloat16):
    values = jax.random.normal(rng, dims, jnp.float32) * deviation
    if len(cuts) > 0:
        values = steps_of(rng, dims, cuts, -0.22, 0.18) * values
    return jnp.clip(values, min=-reach, max=reach).astype(kind)


def setup_inputs(seed: int = 0) -> dict:
    keys = jax.random.split(jax.random.key(seed), 19)
    return {
        "hidden": normal_values(keys[0], (2, TOKENS, D), 1.0, 6.0, ((1, 8),)),
        "w_inner": normal_values(keys[1], (2, D, 2, INNER), D ** -0.5, 0.125, ((3, 4),)),
        "w_state": normal_values(keys[2], (2, D, 2, STATE), D ** -0.5, 0.125),
        "w_step": normal_values(keys[3], (2, D, HEADS), D ** -0.5, 0.125, ((2, 4),)),
        "step_bias": jnp.clip(-5.0 + 3.0 * jax.random.uniform(keys[4], (2, HEADS), jnp.float32) ** steps_of(keys[4], (2, HEADS), ((1, 4),), -0.2, 0.2), -5.0, -2.0),
        "rate": jnp.clip(jnp.exp(math.log(1.5) - 5.0106353 * jax.random.uniform(keys[5], (2, HEADS), jnp.float32) ** steps_of(keys[5], (2, HEADS), ((1, 4),), -0.2, 0.2)), 0.01, 1.5),
        "skip_gain": jnp.clip(0.5 + 1.0 * jax.random.uniform(keys[6], (2, HEADS), jnp.float32) ** steps_of(keys[6], (2, HEADS), ((1, 4),), -0.2, 0.2), 0.5, 1.5),
        "norm_gain": jnp.clip(1.0 + 0.18 * jax.random.normal(keys[7], (2, INNER), jnp.float32), 0.1, 1.9),
        "w_out": normal_values(keys[8], (2, INNER, D), INNER ** -0.5, 0.09375, ((1, 4),)),
        "final_gain": jnp.clip(1.0 + 0.18 * jax.random.normal(keys[9], (2, D), jnp.float32), 0.1, 1.9),
        "head": draw_head(jax.random.fold_in(keys[18], 71), 0),
        "pool": normal_values(keys[11], (2, PAGES, HEADS, HEAD_DIM, STATE), 0.5, 3.0, ((2, 4),)),
        "targets": with_ends(ranked_ids(keys[12], (TOKENS,), VOCAB, 2), jax.random.fold_in(keys[12], 3), 0, VOCAB - 1).astype(jnp.int32),
        "segment_ids": jnp.searchsorted(jnp.cumsum(ragged_sizes(keys[13], NSEQ, TOKENS, MAXLEN, 0)), jnp.arange(TOKENS), side="right").astype(jnp.int32),
        "flags": draw_flags(jax.random.fold_in(keys[18], 71), 0),
        "pages": with_ends(jax.random.randint(keys[15], (NSEQ,), 0, PAGES), jax.random.fold_in(keys[15], 1), 0, PAGES - 1).astype(jnp.int32),
        "live": with_ends((jax.random.randint(keys[16], (NBLK,), 0, 4) < 3).astype(jnp.int32), jax.random.fold_in(keys[16], 1), 0, 1),
        "owners": with_ends(jax.random.randint(keys[17], (NSEQ,), 0, N_SEQ), jax.random.fold_in(keys[17], 1), 0, N_SEQ - 1).astype(jnp.int32),
    }


NORM_EPS = 1e-05
HIGH = lax.Precision.HIGHEST

def block_step(carried, pieces):
    values_in, input_map, output_map, log_decay, step_size, onehot, segment = pieces
    length = values_in.shape[0]
    running = jnp.cumsum(log_decay, axis=0)
    seg_decay = jnp.dot(onehot.T, log_decay, precision=HIGH)
    upto_end = jnp.cumsum(seg_decay, axis=0)
    before = upto_end - seg_decay
    end_rows = jnp.dot(onehot, upto_end, precision=HIGH)
    start_rows = jnp.dot(onehot, before, precision=HIGH)
    places = jnp.arange(length, dtype=jnp.int32)
    allowed = (places[:, None] >= places[None, :]) & (segment[:, None] == segment[None, :])
    log_gap = running.T[:, :, None] - running.T[:, None, :]
    decay_kernel = jnp.exp(jnp.where(allowed[None], log_gap, -jnp.inf))
    scores = jnp.dot(output_map, input_map.T, precision=HIGH)
    weights = decay_kernel * scores[None] * step_size.T[:, None, :]
    mixer_out = jnp.einsum('hts,shp->thp', weights, values_in, precision=HIGH)
    from_state = jnp.einsum('tn,jhpn->tjhp', output_map, carried, precision=HIGH)
    picked = lax.optimization_barrier(jnp.sum(onehot[:, :, None, None] * from_state, axis=1))
    mixer_out = mixer_out + picked * jnp.exp(running - start_rows)[:, :, None]
    retain = jnp.exp(end_rows - running) * step_size
    spread = onehot[:, :, None, None] * (retain[:, None, :, None] * values_in[:, None, :, :])
    added_state = jnp.einsum('tjhp,tn->jhpn', spread, input_map, precision=HIGH)
    carried = jnp.exp(seg_decay)[:, :, None, None] * carried + added_state
    return (carried, mixer_out)

def scan_blocks(values_in, input_map, output_map, log_decay, step_size, onehot, segment, init_state, length):
    turns = values_in.shape[0] // length

    def to_blocks(array):
        return array.reshape((turns, length) + array.shape[1:])
    pieces = tuple((to_blocks(array) for array in (values_in, input_map, output_map, log_decay, step_size, onehot, segment)))
    end_state, outputs = lax.scan(block_step, init_state, pieces)
    return (outputs.reshape(values_in.shape), end_state)

def reference(hidden, w_inner, w_state, w_step, step_bias, rate, skip_gain, norm_gain, w_out, final_gain, head, pool, targets, segment_ids, flags, pages, live, owners):
    seg_onehot = (segment_ids[:, None] == jnp.arange(NSEQ, dtype=jnp.int32)[None, :]).astype(jnp.float32)
    live_rows = jnp.repeat(live.astype(jnp.float32), SPAN)
    group_width = INNER // N_VOCAB
    scores_list = []
    for which_model in range(2):
        tokens_in = hidden[which_model]
        inner_proj = jnp.dot(tokens_in, w_inner[which_model].reshape(D, 2 * INNER), preferred_element_type=jnp.float32)
        gate_in = inner_proj[:, :INNER]
        values_bf = jax.nn.silu(inner_proj[:, INNER:]).astype(jnp.bfloat16)
        values_in = lax.optimization_barrier(values_bf).astype(jnp.float32).reshape(TOKENS, HEADS, HEAD_DIM)
        state_bf = jax.nn.silu(jnp.dot(tokens_in, w_state[which_model].reshape(D, 2 * STATE), preferred_element_type=jnp.float32)).astype(jnp.bfloat16)
        state_proj = lax.optimization_barrier(state_bf).astype(jnp.float32)
        step_size = jax.nn.softplus(jnp.dot(tokens_in, w_step[which_model], preferred_element_type=jnp.float32) + step_bias[which_model][None, :])
        log_decay = -step_size * rate[which_model][None, :]
        init_state = pool[which_model][pages].astype(jnp.float32) * flags.astype(jnp.float32)[:, None, None, None]
        mixer_out, end_state = scan_blocks(values_in, state_proj[:, :STATE], state_proj[:, STATE:], log_decay, step_size, seg_onehot, segment_ids, init_state, SPAN)
        mixer_out = mixer_out + skip_gain[which_model][None, :, None] * values_in
        gated_rows = mixer_out.reshape(TOKENS, INNER) * jax.nn.silu(gate_in)
        mean_square = lax.optimization_barrier(jnp.mean(gated_rows * gated_rows, axis=1, keepdims=True))
        mixed_rows = (gated_rows * lax.rsqrt(mean_square + NORM_EPS) * norm_gain[which_model][None, :]).astype(jnp.bfloat16)
        weights_out = w_out[which_model]

        def add_group(running, group_index):
            part_rows = lax.dynamic_slice_in_dim(mixed_rows, group_index * group_width, group_width, 1)
            part_weights = lax.dynamic_slice_in_dim(weights_out, group_index * group_width, group_width, 0)
            rounded = lax.optimization_barrier(jnp.dot(part_rows, part_weights, preferred_element_type=jnp.float32).astype(jnp.bfloat16))
            return (running + rounded.astype(jnp.float32), None)
        out_sum, unused = lax.scan(add_group, jnp.zeros((TOKENS, D), jnp.float32), jnp.arange(N_VOCAB, dtype=jnp.int32))
        residual = tokens_in.astype(jnp.float32) + out_sum
        normed = (residual * lax.rsqrt(lax.optimization_barrier(jnp.mean(residual * residual, axis=1, keepdims=True)) + NORM_EPS) * final_gain[which_model][None, :]).astype(jnp.bfloat16)
        head_model = head[which_model]

        def block_score(pieces):
            row_block, target_block = pieces
            logits = jnp.dot(row_block, head_model, preferred_element_type=jnp.float32)
            row_top = lax.optimization_barrier(jnp.max(logits, axis=1))
            row_total = lax.optimization_barrier(jnp.sum(jnp.exp(logits - row_top[:, None]), axis=1))
            chosen = jnp.take_along_axis(logits, target_block[:, None], axis=1)[:, 0]
            return chosen - row_top - jnp.log(row_total)
        scored = lax.map(block_score, (normed.reshape(NBLK, SPAN, D), targets.reshape(NBLK, SPAN)))
        scores_list.append(scored.reshape(TOKENS))
    token_diff = live_rows * (scores_list[0] - scores_list[1])
    per_sequence = jnp.dot(seg_onehot.T, token_diff, precision=HIGH)
    owner_onehot = (owners[None, :] == jnp.arange(N_SEQ, dtype=jnp.int32)[:, None]).astype(jnp.float32)
    owned = owner_onehot * per_sequence[None, :]
    return (token_diff, owned)
```

```python
import jax
import jax.numpy as jnp
from jax import lax
from jax.sharding import PartitionSpec as P

SPAN = 256


NORM_EPS = 1e-05
HIGH = lax.Precision.HIGHEST


def front(tokens_in, w_in, w_st, w_dt, bias, rate, lower, seg_onehot, last_rows):
    rows = tokens_in.shape[0]
    heads = rate.shape[0]
    width = w_in.shape[2]
    gate_in = jnp.dot(tokens_in, w_in[0], preferred_element_type=jnp.float32)
    values = jax.nn.silu(
        jnp.dot(tokens_in, w_in[1], preferred_element_type=jnp.float32)
    ).astype(jnp.bfloat16)
    input_map = jax.nn.silu(
        jnp.dot(tokens_in, w_st[0], preferred_element_type=jnp.float32)
    ).astype(jnp.bfloat16)
    output_map = jax.nn.silu(
        jnp.dot(tokens_in, w_st[1], preferred_element_type=jnp.float32)
    ).astype(jnp.bfloat16)
    step_size = jax.nn.softplus(
        jnp.dot(tokens_in, w_dt, preferred_element_type=jnp.float32) + bias[None, :]
    )
    log_decay = -step_size * rate[None, :]
    running = jnp.dot(lower, log_decay, precision=HIGH)
    seg_decay = jnp.dot(seg_onehot.T, log_decay, precision=HIGH)
    retain = jnp.exp(running[-1:] - running) * step_size * last_rows[:, None]
    spread = (
        retain[:, :, None] * values.astype(jnp.float32).reshape(rows, heads, width // heads)
    ).astype(jnp.bfloat16)
    state = lax.dot_general(
        spread.reshape(rows, width),
        input_map,
        (((0,), (0,)), ((), ())),
        preferred_element_type=jnp.float32,
    ).astype(jnp.bfloat16)
    return gate_in, values, input_map, output_map, step_size, running, seg_decay, state


def within(values, input_map, output_map, step_size, running, allowed):
    rows, width = values.shape
    heads = running.shape[1]
    scores = jnp.dot(output_map, input_map.T, preferred_element_type=jnp.float32)
    across = running.T
    log_gap = across[:, :, None] - across[:, None, :]
    decay_kernel = jnp.exp(jnp.where(allowed[None], log_gap, -jnp.inf))
    weights = (decay_kernel * (scores[None] * step_size.T[:, None, :])).astype(jnp.bfloat16)
    by_head = values.reshape(rows, heads, width // heads)
    return jnp.einsum("hts,shp->thp", weights, by_head, preferred_element_type=jnp.float32)


def per_device(
    hidden,
    w_inner,
    w_state,
    w_step,
    step_bias,
    rate,
    skip_gain,
    norm_gain,
    w_out,
    final_gain,
    head,
    pool,
    targets,
    segment_ids,
    flags,
    pages,
    live,
    owners,
):
    row_count = targets.shape[0]
    seq_count = flags.shape[0]
    head_count = rate.shape[1]
    head_width = pool.shape[3]
    state_width = pool.shape[4]
    inner_local = w_inner.shape[3]
    inner_total = inner_local * lax.axis_size("vocab")
    vocab_local = head.shape[2]
    devices = lax.axis_size("seq")
    here = lax.axis_index("seq")
    sequences = jnp.arange(seq_count, dtype=jnp.int32)
    seg_onehot = (segment_ids[:, None] == sequences[None, :]).astype(jnp.float32)
    first_id = segment_ids[0]
    last_id = segment_ids[row_count - 1]
    first_rows = (segment_ids == first_id).astype(jnp.float32)
    last_rows = (segment_ids == last_id).astype(jnp.float32)
    places = jnp.arange(row_count, dtype=jnp.int32)
    causal = places[:, None] >= places[None, :]
    lower = causal.astype(jnp.float32)
    allowed = causal & (segment_ids[:, None] == segment_ids[None, :])
    live_rows = jnp.repeat(live.astype(jnp.float32), SPAN)
    target_local = targets - lax.axis_index("vocab") * vocab_local
    hits = target_local[:, None] == jnp.arange(vocab_local, dtype=jnp.int32)[None, :]
    flag_rows = seg_onehot * flags.astype(jnp.float32)[None, :]
    order = jnp.arange(devices, dtype=jnp.int32)

    w_inner = lax.optimization_barrier(jnp.transpose(w_inner, (0, 2, 1, 3)))
    w_state = lax.optimization_barrier(jnp.transpose(w_state, (0, 2, 1, 3)))
    fronts = [
        front(
            hidden[m], w_inner[m], w_state[m], w_step[m], step_bias[m], rate[m],
            lower, seg_onehot, last_rows,
        )
        for m in range(2)
    ]
    small = jnp.concatenate(
        [
            jnp.stack([fronts[0][6], fronts[1][6]]).reshape(-1),
            jnp.broadcast_to(last_id.astype(jnp.float32), (1,)),
        ]
    )
    small = jnp.pad(small, (0, -small.shape[0] % 1024)).reshape(-1, 128)
    small_all = lax.all_gather(small, "seq").reshape(devices, -1)
    states_all = [lax.all_gather(fronts[m][7], "seq") for m in range(2)]
    count = 2 * seq_count * head_count
    decay_all = small_all[:, :count].reshape(devices, 2, seq_count, head_count)
    last_all = small_all[:, count]
    first_onehot = (sequences == first_id).astype(jnp.float32)
    first_decay = jnp.sum(decay_all * first_onehot[None, None, :, None], axis=2)
    first_decay = jnp.where((order < here)[:, None, None], first_decay, 0.0)
    prior_total = jnp.sum(first_decay, axis=0)
    later = (order[None, :] > order[:, None]).astype(jnp.float32)
    after = jnp.sum(later[:, :, None, None] * first_decay[None], axis=1)
    used = (order < here) & (last_all == first_id.astype(jnp.float32))
    coef = jnp.where(used[:, None, None], jnp.exp(after), 0.0)

    sums = []
    for m in range(2):
        if m == 1:
            later_front, first_part = lax.optimization_barrier((fronts[1], sums[0][0]))
            fronts[1], sums[0] = later_front, (first_part, sums[0][1])
        gate_in, values, input_map, output_map, step_size, running, seg_decay, state = fronts[m]
        mixer_out = within(values, input_map, output_map, step_size, running, allowed)
        before = jnp.cumsum(seg_decay, axis=0) - seg_decay
        start_rows = jnp.dot(seg_onehot, before, precision=HIGH)
        from_first = jnp.exp(running)
        from_start = jnp.exp(running - start_rows + first_rows[:, None] * prior_total[m][None, :])
        reads = output_map.astype(jnp.float32)
        picked = jnp.zeros((row_count, inner_local), jnp.float32)
        for j in range(seq_count):
            page = lax.dynamic_slice(pool, (m, pages[j], 0, 0, 0), (1, 1) + pool.shape[2:])
            picked = picked + lax.dot_general(
                (reads * flag_rows[:, j : j + 1]).astype(jnp.bfloat16),
                page.reshape(inner_local, state_width),
                (((1,), (1,)), ((), ())),
                preferred_element_type=jnp.float32,
            )
        received = states_all[m].astype(jnp.float32).reshape(
            devices, head_count, head_width, state_width
        )
        prior = jnp.sum(received * coef[:, m, :, None, None], axis=0).astype(jnp.bfloat16)
        carried = lax.dot_general(
            (reads * first_rows[:, None]).astype(jnp.bfloat16),
            prior.reshape(inner_local, state_width),
            (((1,), (1,)), ((), ())),
            preferred_element_type=jnp.float32,
        )
        by_head = (row_count, head_count, head_width)
        mixer_out = (
            mixer_out
            + picked.reshape(by_head) * from_start[:, :, None]
            + carried.reshape(by_head) * from_first[:, :, None]
            + skip_gain[m][None, :, None] * values.astype(jnp.float32).reshape(by_head)
        )
        gated_rows = mixer_out.reshape(row_count, inner_local) * jax.nn.silu(gate_in)
        square_sum = lax.psum(jnp.sum(gated_rows * gated_rows, axis=1), "vocab")
        mixed_rows = (gated_rows * norm_gain[m][None, :]).astype(jnp.bfloat16)
        out_part = jnp.dot(mixed_rows, w_out[m], preferred_element_type=jnp.float32)
        sums.append((out_part.astype(jnp.bfloat16), square_sum))
    first_sum = lax.psum(sums[0][0], "vocab")
    first_sum, second_part = lax.optimization_barrier((first_sum, sums[1][0]))
    out_sums = [first_sum, lax.psum(second_part, "vocab")]
    row_stats = []
    for m in range(2):
        out_sum = out_sums[m]
        if m == 1:
            out_sum, row_stats = lax.optimization_barrier((out_sum, row_stats))
        out_sum = out_sum.astype(jnp.float32)
        square_sum = sums[m][1]
        out_sum = out_sum * lax.rsqrt(square_sum / inner_total + NORM_EPS)[:, None]
        residual = hidden[m].astype(jnp.float32) + out_sum
        normed = (
            residual
            * lax.rsqrt(jnp.mean(residual * residual, axis=1, keepdims=True) + NORM_EPS)
            * final_gain[m][None, :]
        ).astype(jnp.bfloat16)
        logits = jnp.dot(normed, head[m], preferred_element_type=jnp.float32)
        row_top = jnp.max(logits, axis=1)
        row_stats.append(row_top)
        row_stats.append(jnp.sum(jnp.exp(logits - row_top[:, None]), axis=1))
        row_stats.append(jnp.sum(jnp.where(hits, logits, 0.0), axis=1))
    stats = lax.all_gather(jnp.stack(row_stats), "vocab")
    scores = []
    for m in range(2):
        tops = stats[:, 3 * m]
        top = jnp.max(tops, axis=0)
        total = jnp.sum(stats[:, 3 * m + 1] * jnp.exp(tops - top[None]), axis=0)
        scores.append(jnp.sum(stats[:, 3 * m + 2], axis=0) - top - jnp.log(total))
    token_diff = live_rows * (scores[0] - scores[1])
    per_sequence = jnp.sum(seg_onehot * token_diff[:, None], axis=0)
    totals = lax.psum(per_sequence, "seq")
    owned = jnp.where(owners == here, totals, 0.0)[None, :]
    return (token_diff, owned)


def solution(mesh):
    placed = (
        P(None, "seq", None),
        P(None, None, None, "vocab"),
        P(),
        P(None, None, "vocab"),
        P(None, "vocab"),
        P(None, "vocab"),
        P(None, "vocab"),
        P(None, "vocab"),
        P(None, "vocab", None),
        P(),
        P(None, None, "vocab"),
        P(None, None, "vocab", None, None),
        P("seq"),
        P("seq"),
        P(),
        P(),
        P("seq"),
        P(),
    )
    return jax.shard_map(
        per_device,
        mesh=mesh,
        in_specs=placed,
        out_specs=(P("seq"), P("seq", None)),
        check_vma=False,
    )
```
